256 devices in a mesh: mp: 8 (over z), hidden: 32 (over y, x, core).
Axes of the slice: x: 4, y: 4, z: 8, core: 2. Of those that a mesh axis runs over, the one named last changes fastest.
Arguments:
- inputs: bfloat16 [768, 18432], P('hidden', 'mp'), may hold values from -6 to 6
- gate_weight: bfloat16 [18432, 12288], P('mp', 'hidden'), may hold values from -0.046875 to 0.046875
- up_weight: bfloat16 [18432, 12288], P('mp', 'hidden'), may hold values from -0.046875 to 0.046875
- down_weight: bfloat16 [12288, 18432], P('hidden', 'mp'), may hold values from -0.0546875 to 0.0546875
- cotangent: bfloat16 [768, 18432], P('hidden', 'mp'), may hold values from -6 to 6
Outputs:
- grad_inputs: bfloat16 [768, 18432], P('hidden', 'mp')
- grad_gate: bfloat16 [18432, 12288], P('mp', 'hidden')
- grad_up: bfloat16 [18432, 12288], P('mp', 'hidden')
- grad_down: bfloat16 [12288, 18432], P('hidden', 'mp')
The draws below stay inside these ranges and needn't reach their ends.
All inputs are finite; a program needn't handle non-finite values.
Results may differ from the reference program's by a relative error of at most 0.02.
Values may be sent and summed in bfloat16 or wider, within the bound.
A program may use at most 128 MiB of HBM per device.

```python
import jax
import jax.numpy as jnp
from jax import lax

D = 18432
TOKENS = 768
FF = 12288


def block_levels(rng, dims, cuts, least, top_value):
    factor_of, own = 1.0, jax.random.fold_in(rng, 6)
    for position, blocks in cuts:
        draws = jnp.exp(jax.random.uniform(jax.random.fold_in(own, position), (blocks,), jnp.float32, least / len(cuts), top_value / len(cuts)))
        factor_of = factor_of * jnp.repeat(draws, dims[position] // blocks).reshape([-1 if axis == position else 1 for axis in range(len(dims))])
    return factor_of


def bell_draw(rng, dims, deviation, most, split=(), kind=jnp.bfloat16):
    loudness = block_levels(rng, dims, split, -0.22, 0.18) if split else 1.0
    values = jax.random.normal(rng, dims, jnp.float32) * deviation * loudness
    return jnp.minimum(jnp.maximum(values, -most), most).astype(kind)


def setup_inputs(seed: int = 0) -> dict:
    arg_keys = jax.random.split(jax.random.key(seed), 6)
    return {
        "inputs": bell_draw(arg_keys[0], (TOKENS, D), 1.0, 6.0, ((0, 32), (1, 8))),
        "gate_weight": bell_draw(arg_keys[1], (D, FF), D ** -0.5, 0.046875, ((0, 8), (1, 32))),
        "up_weight": bell_draw(arg_keys[2], (D, FF), D ** -0.5, 0.046875, ((0, 8), (1, 32))),
        "down_weight": bell_draw(arg_keys[3], (FF, D), FF ** -0.5, 0.0546875, ((0, 32), (1, 8))),
        "cotangent": bell_draw(arg_keys[4], (TOKENS, D), 1.0, 6.0, ((0, 32), (1, 8))),
    }


def reference(inputs, gate_weight, up_weight, down_weight, cotangent):
    gate = jnp.dot(inputs, gate_weight, preferred_element_type=jnp.float32)
    up = jnp.dot(inputs, up_weight, preferred_element_type=jnp.float32)
    dhid = lax.dot_general(cotangent, down_weight, (((1,), (1,)), ((), ())), preferred_element_type=jnp.float32)
    sig = jax.nn.sigmoid(gate)
    hidden_act = (gate * sig * up).astype(jnp.bfloat16)
    dup = (dhid * gate * sig).astype(jnp.bfloat16)
    dgate = (dhid * up * sig * (1.0 + gate * (1.0 - sig))).astype(jnp.bfloat16)
    grad_down = lax.dot_general(hidden_act, cotangent, (((0,), (0,)), ((), ())), preferred_element_type=jnp.float32).astype(jnp.bfloat16)
    grad_gate = lax.dot_general(inputs, dgate, (((0,), (0,)), ((), ())), preferred_element_type=jnp.float32).astype(jnp.bfloat16)
    grad_up = lax.dot_general(inputs, dup, (((0,), (0,)), ((), ())), preferred_element_type=jnp.float32).astype(jnp.bfloat16)
    grad_inputs = lax.dot_general(dgate, gate_weight, (((1,), (1,)), ((), ())), preferred_element_type=jnp.float32)
    grad_inputs = grad_inputs + lax.dot_general(dup, up_weight, (((1,), (1,)), ((), ())), preferred_element_type=jnp.float32)
    return grad_inputs.astype(jnp.bfloat16), grad_gate, grad_up, grad_down
```

```python
import functools

import jax
import jax.numpy as jnp
from jax import lax
from jax.experimental import pallas as pl
from jax.experimental.pallas import tpu as pltpu
from jax.sharding import PartitionSpec as P

MESH = pl.DeviceIdType.MESH
F32, BF16 = jnp.float32, jnp.bfloat16

NX, NY, NZ = 4, 4, 8
PIECE = 48
SHARD = 24
DM = 2304
HALF = DM // 2
FD = 384
CHUNKS = 4
PER = 4
ROWS = PIECE * PER
BLK = ROWS // NZ

XR, XL, YU, YD = (1, 0), (-1, 0), (0, 1), (0, -1)

GATHER = (
    ((1, 0), XR), ((-1, 0), XL), ((0, 1), YU), ((0, -1), YD),
    ((2, 0), XR), ((-1, -1), XL), ((0, 2), YU), ((1, -1), YD),
    ((1, 1), XR), ((2, -1), XL), ((-1, 1), YU), ((-1, 2), YD),
    ((1, 2), XR), ((2, 1), XL), ((2, 2), YD),
)
REDUCE = {
    (1, 0): XR, (2, 0): XR, (1, -1): XR, (1, 1): XR,
    (-1, 0): XL, (-1, -1): XL, (-1, 2): XL,
    (0, 1): YU, (0, 2): YU, (2, 1): YU, (-1, 1): YU,
    (0, -1): YD, (2, 2): YD, (2, -1): YD, (1, 2): YD,
}
CHUNK_PIECES = (
    ((0, 0), (1, 0), (-1, 0), (0, 1)),
    ((2, 0), (-1, -1), (0, 2), (1, -1)),
    ((2, 1), (2, 2), (1, 2), (2, -1)),
    ((0, -1), (1, 1), (-1, 1), (-1, 2)),
)
SLOT = {p: i for i, p in enumerate(p for chunk in CHUNK_PIECES for p in chunk)}


def less(p, d):
    return tuple((a - b + 1) % 4 - 1 for a, b in zip(p, d))


SOURCE = {p: less(p, d) for p, d in GATHER}
PARENT = {p: less(p, d) for p, d in REDUCE.items()}
CHILDREN = {p: [q for q in REDUCE if PARENT[q] == p] for p in SLOT}
NT = (((1,), (1,)), ((), ()))
TN = (((0,), (0,)), ((), ()))


def dot(a, b, dims=(((1,), (0,)), ((), ()))):
    return lax.dot_general(a, b, dims, preferred_element_type=F32)


def kernel(
    x_hbm, wg_hbm, wu_hbm, wd_hbm, c_hbm,
    gi_hbm, gg_hbm, gu_hbm, gd_hbm,
    own, stage, xc, wcat, wd, part, rs_s, rs_r, agb, act,
    gi_own, gi_s, gi_r, tr_s, tr_r, fin, acc_gu, acc_d, out_gu, out_d,
    load_sem, stage_sem, ag_ss, ag_rs, sib_ss, sib_rs, rs_ss, rs_rs, za_ss, za_rs,
    gx_ss, gx_rs, tr_ss, tr_rs, fin_sem, out_sem,
):
    z = lax.axis_index("mp")
    h = lax.axis_index("hidden")
    c = lax.rem(h, 2)
    chip = h // 2
    x, y = lax.rem(chip, NX), chip // NX

    def at(d):
        nx, ny = lax.rem(x + d[0] + NX, NX), lax.rem(y + d[1] + NY, NY)
        return {"hidden": (ny * NX + nx) * 2 + c}

    sibling = {"hidden": h + 1 - 2 * c}

    def zat(o):
        return lax.rem(z + o + 2 * NZ, NZ)

    def send(src, dst, ss, rs, dev):
        return pltpu.make_async_remote_copy(
            src_ref=src, dst_ref=dst, send_sem=ss, recv_sem=rs, device_id=dev, device_id_type=MESH
        )

    sent = []

    def start(copy):
        copy.start()
        sent.append(copy)

    loads = [
        pltpu.make_async_copy(x_hbm, own.at[0], load_sem.at[0]),
        pltpu.make_async_copy(c_hbm, own.at[1], load_sem.at[1]),
        pltpu.make_async_copy(wg_hbm, wcat.at[:, pl.ds(0, FD)], load_sem.at[2]),
        pltpu.make_async_copy(wu_hbm, wcat.at[:, pl.ds(FD, FD)], load_sem.at[3]),
        pltpu.make_async_copy(wd_hbm, wd, load_sem.at[4]),
    ]
    for copy in loads:
        copy.start()

    barrier = pltpu.get_barrier_semaphore()
    for dev in (at(XR), at(XL), at(YU), at(YD), {"mp": zat(1)}, {"mp": zat(-1)}, sibling):
        pl.semaphore_signal(barrier, inc=1, device_id=dev, device_id_type=MESH)
    pl.semaphore_wait(barrier, 7)

    loads[0].wait()
    loads[1].wait()
    swap = send(own.at[1 - c], stage, stage_sem.at[0], stage_sem.at[1], sibling)
    start(swap)
    swap.wait_recv()
    mine, other = own[c].astype(F32), stage[...].astype(F32)
    first = c == 0
    xc[c, SLOT[0, 0]] = jnp.concatenate(
        [jnp.where(first, mine, other), jnp.where(first, other, mine)], axis=0
    ).astype(BF16)

    def share(p):
        s = SLOT[p]
        return send(xc.at[c, s], xc.at[c, s], sib_ss.at[s], sib_rs.at[s], sibling)

    def hop(p, d):
        s = SLOT[p]
        return send(
            xc.at[c, SLOT[SOURCE[p]]], xc.at[c, s], ag_ss.at[s], ag_rs.at[s], at((-d[0], -d[1]))
        )

    def forward(q):
        for p, d in GATHER:
            if SOURCE[p] == q:
                start(hop(p, d))

    def arrive(p, d):
        hop(p, d).wait_recv()
        forward(p)
        start(share(p))

    def gather_step(t):
        for p, d in GATHER[4 * t : 4 * t + 4]:
            arrive(p, d)

    forward((0, 0))
    start(share((0, 0)))

    def rows_of(a, k):
        return xc[a, pl.ds(PER * k, PER)].reshape(ROWS, DM)

    def products(k):
        for p in CHUNK_PIECES[k]:
            s = SLOT[p]
            send(xc.at[1 - c, s], xc.at[1 - c, s], sib_ss.at[s], sib_rs.at[s], sibling).wait_recv()

        def tile(n, _):
            cols = pl.ds(pl.multiple_of(n * 256, 256), 256)
            part[k, :, :, cols] = dot(rows_of(0, k), wcat[:, cols]).reshape(NZ, BLK, 256)
            return 0

        lax.fori_loop(0, 3, tile, 0)
        part[k, :, :, pl.ds(2 * FD, FD)] = dot(rows_of(1, k), wd[...], NT).reshape(NZ, BLK, FD)

    def sign(k):
        return 1 if k % 2 == 0 else -1

    def rs_copy(k, m):
        to = sign(k) if m < 4 else -sign(k)
        return send(rs_s.at[k, m], rs_r.at[k, m], rs_ss.at[k, m], rs_rs.at[k, m], {"mp": zat(to)})

    def rs_send(k, m):
        owner = sign(k) * (4 - m) if m < 4 else -sign(k) * (7 - m)
        value = part[k, zat(owner)]
        if m not in (0, 4):
            rs_copy(k, m - 1).wait_recv()
            value = value + rs_r[k, m - 1].astype(F32)
        rs_s[k, m] = value.astype(BF16)
        start(rs_copy(k, m))

    def za_copy(k, m):
        to = -sign(k) if m < 4 else sign(k)
        hops = m if m < 4 else m - 4
        block = agb.at[k, zat(-to * hops)]
        return send(block, block, za_ss.at[k, m], za_rs.at[k, m], {"mp": zat(to)})

    def za_wait(k, m):
        to = -sign(k) if m < 4 else sign(k)
        hops = m if m < 4 else m - 4
        block = agb.at[k, zat(-to * (hops + 1))]
        send(block, block, za_ss.at[k, m], za_rs.at[k, m], {"mp": zat(to)}).wait_recv()

    def activate(k):
        rs_copy(k, 3).wait_recv()
        rs_copy(k, 6).wait_recv()
        total = part[k, z] + rs_r[k, 3].astype(F32) + rs_r[k, 6].astype(F32)
        gate, up, dhid = total[:, :FD], total[:, FD : 2 * FD], total[:, 2 * FD :]
        sig = jax.nn.sigmoid(gate)
        agb[k, z] = jnp.concatenate(
            [
                gate * sig * up,
                dhid * up * sig * (1.0 + gate * (1.0 - sig)),
                dhid * gate * sig,
            ],
            axis=1,
        ).astype(BF16)
        start(za_copy(k, 0))
        start(za_copy(k, 4))

    def z_step(k, i):
        if i < 4:
            rs_send(k, i)
            if i < 3:
                rs_send(k, 4 + i)
        elif i == 4:
            activate(k)
        elif i < 8:
            za_wait(k, i - 5)
            start(za_copy(k, i - 4))
            za_wait(k, i - 1)
            if i < 7:
                start(za_copy(k, i))
        else:
            za_wait(k, 3)
            act[k] = jnp.concatenate([agb[k, j].astype(F32) for j in range(NZ)], axis=0).astype(BF16)

    def gi_swap(k):
        s = pl.ds(PER * k, PER)
        return send(gi_s.at[s], gi_r.at[s], gx_ss.at[k], gx_rs.at[k], sibling)

    def input_grad(k):
        slots = pl.ds(PER * k, PER)

        def tile(n, half, dst):
            rows = pl.ds(pl.multiple_of(half * HALF + n * FD, 128), FD)
            cols = pl.ds(pl.multiple_of(n * FD, 128), FD)
            value = dot(act[k, :, pl.ds(FD, 2 * FD)], wcat[rows, :], NT)
            dst[slots, :, cols] = value.reshape(PER, PIECE, FD).astype(dst.dtype)
            return 0

        lax.fori_loop(0, 3, lambda n, _: tile(n, 1 - c, gi_s), 0)
        start(gi_swap(k))
        lax.fori_loop(0, 3, lambda n, _: tile(n, c, gi_own), 0)

    def tr_copy(p):
        s = SLOT[p]
        return send(tr_s.at[s], tr_r.at[s], tr_ss.at[s], tr_rs.at[s], at(REDUCE[p]))

    def tree_sum(p):
        s = SLOT[p]
        value = gi_own[s] + gi_r[s].astype(F32)
        for q in CHILDREN[p]:
            tr_copy(q).wait_recv()
            value = value + tr_r[SLOT[q]].astype(F32)
        return value

    def tree(*pieces):
        for p in pieces:
            tr_s[SLOT[p]] = tree_sum(p).astype(BF16)
            start(tr_copy(p))

    outs = []

    def weight_grads(k):
        last = k == CHUNKS - 1
        slots = pl.ds(PER * k, PER)

        def gu_tile(n, _):
            cols = pl.ds(pl.multiple_of(n * 256, 256), 256)
            value = dot(xc[0, slots, :, cols].reshape(ROWS, 256), act[k, :, pl.ds(FD, 2 * FD)], TN)
            if k:
                value = value + acc_gu[cols, :]
            if last:
                out_gu[cols, :] = value.astype(BF16)
            else:
                acc_gu[cols, :] = value
            return 0

        def d_tile(n, _):
            cols = pl.ds(pl.multiple_of(n * 256, 256), 256)
            value = dot(act[k, :, pl.ds(0, FD)], xc[1, slots, :, cols].reshape(ROWS, 256), TN)
            if k:
                value = value + acc_d[:, cols]
            if last:
                out_d[:, cols] = value.astype(BF16)
            else:
                acc_d[:, cols] = value
            return 0

        lax.fori_loop(0, DM // 256, gu_tile, 0)
        if last:
            outs.append(pltpu.make_async_copy(out_gu.at[:, pl.ds(0, FD)], gg_hbm, out_sem.at[0]))
            outs.append(pltpu.make_async_copy(out_gu.at[:, pl.ds(FD, FD)], gu_hbm, out_sem.at[1]))
            outs[0].start()
            outs[1].start()
        lax.fori_loop(0, DM // 256, d_tile, 0)
        if last:
            outs.append(pltpu.make_async_copy(out_d, gd_hbm, out_sem.at[2]))
            outs[2].start()

    gather_step(0)
    for copy in loads[2:]:
        copy.wait()
    products(0)
    z_step(0, 0)
    gather_step(1)
    z_step(0, 1)
    products(1)
    z_step(0, 2)
    z_step(1, 0)
    gather_step(2)
    z_step(0, 3)
    z_step(1, 1)
    gather_step(3)
    z_step(0, 4)
    z_step(1, 2)
    products(2)
    z_step(0, 5)
    z_step(1, 3)
    z_step(2, 0)
    products(3)
    z_step(0, 6)
    z_step(1, 4)
    z_step(2, 1)
    z_step(3, 0)
    z_step(0, 7)
    z_step(1, 5)
    z_step(2, 2)
    z_step(3, 1)
    z_step(0, 8)
    input_grad(0)
    z_step(1, 6)
    z_step(2, 3)
    z_step(3, 2)
    weight_grads(0)
    z_step(1, 7)
    z_step(2, 4)
    z_step(3, 3)
    gi_swap(0).wait_recv()
    z_step(1, 8)
    input_grad(1)
    z_step(2, 5)
    z_step(3, 4)
    gi_swap(1).wait_recv()
    tree((-1, -1))
    z_step(2, 6)
    z_step(3, 5)
    weight_grads(1)
    z_step(2, 7)
    z_step(3, 6)
    z_step(2, 8)
    input_grad(2)
    z_step(3, 7)
    gi_swap(2).wait_recv()
    tree((2, 2), (2, 1), (1, 2))
    z_step(3, 8)
    input_grad(3)
    tree((2, -1), (1, -1))
    gi_swap(3).wait_recv()
    tree((1, 1), (-1, 1), (-1, 2))
    tree((2, 0), (0, -1))
    weight_grads(2)
    tree((1, 0), (-1, 0), (0, 2))
    tree((0, 1))
    weight_grads(3)

    gi_own[SLOT[0, 0]] = tree_sum((0, 0))
    theirs = pl.ds(pl.multiple_of((1 - c) * SHARD, 8), SHARD)
    ours = pl.ds(pl.multiple_of(c * SHARD, 8), SHARD)
    fin[2] = gi_own[SLOT[0, 0], theirs, :].astype(BF16)
    last = send(fin.at[2], fin.at[1], fin_sem.at[0], fin_sem.at[1], sibling)
    start(last)
    fin[0] = gi_own[SLOT[0, 0], ours, :].astype(BF16)
    half_c = pl.ds(pl.multiple_of(c * HALF, 128), HALF)
    half_o = pl.ds(pl.multiple_of((1 - c) * HALF, 128), HALF)
    outs.append(pltpu.make_async_copy(fin.at[0], gi_hbm.at[:, half_c], out_sem.at[3]))
    outs[3].start()
    last.wait_recv()
    outs.append(pltpu.make_async_copy(fin.at[1], gi_hbm.at[:, half_o], out_sem.at[4]))
    outs[4].start()

    for copy in outs:
        copy.wait()
    for copy in sent:
        copy.wait_send()


def shards(inputs, gate_weight, up_weight, down_weight, cotangent):
    dma = pltpu.SemaphoreType.DMA
    any_spec = pl.BlockSpec(memory_space=pl.ANY)
    slots = CHUNKS * PER
    return pl.pallas_call(
        kernel,
        out_shape=(
            jax.ShapeDtypeStruct((SHARD, DM), BF16),
            jax.ShapeDtypeStruct((DM, FD), BF16),
            jax.ShapeDtypeStruct((DM, FD), BF16),
            jax.ShapeDtypeStruct((FD, DM), BF16),
        ),
        in_specs=[any_spec] * 5,
        out_specs=(any_spec,) * 4,
        scratch_shapes=[
            pltpu.VMEM((2, SHARD, DM), BF16),
            pltpu.VMEM((SHARD, DM), BF16),
            pltpu.VMEM((2, slots, PIECE, DM), BF16),
            pltpu.VMEM((DM, 2 * FD), BF16),
            pltpu.VMEM((FD, DM), BF16),
            pltpu.VMEM((CHUNKS, NZ, BLK, 3 * FD), F32),
            pltpu.VMEM((CHUNKS, 7, BLK, 3 * FD), BF16),
            pltpu.VMEM((CHUNKS, 7, BLK, 3 * FD), BF16),
            pltpu.VMEM((CHUNKS, NZ, BLK, 3 * FD), BF16),
            pltpu.VMEM((CHUNKS, ROWS, 3 * FD), BF16),
            pltpu.VMEM((slots, PIECE, HALF), F32),
            pltpu.VMEM((slots, PIECE, HALF), BF16),
            pltpu.VMEM((slots, PIECE, HALF), BF16),
            pltpu.VMEM((slots, PIECE, HALF), BF16),
            pltpu.VMEM((slots, PIECE, HALF), BF16),
            pltpu.VMEM((3, SHARD, HALF), BF16),
            pltpu.VMEM((DM, 2 * FD), F32),
            pltpu.VMEM((FD, DM), F32),
            pltpu.VMEM((DM, 2 * FD), BF16),
            pltpu.VMEM((FD, DM), BF16),
            dma((5,)),
            dma((2,)),
            dma((slots,)), dma((slots,)),
            dma((slots,)), dma((slots,)),
            dma((CHUNKS, 7)), dma((CHUNKS, 7)),
            dma((CHUNKS, 7)), dma((CHUNKS, 7)),
            dma((CHUNKS,)), dma((CHUNKS,)),
            dma((slots,)), dma((slots,)),
            dma((2,)),
            dma((5,)),
        ],
        compiler_params=pltpu.CompilerParams(
            collective_id=0, has_side_effects=True, vmem_limit_bytes=60 * 1024 * 1024
        ),
    )(inputs, gate_weight, up_weight, down_weight, cotangent)


def solution(mesh):
    placed = (
        P("hidden", "mp"),
        P("mp", "hidden"),
        P("mp", "hidden"),
        P("hidden", "mp"),
        P("hidden", "mp"),
    )
    return jax.shard_map(
        shards,
        mesh=mesh,
        in_specs=placed,
        out_specs=(P("hidden", "mp"), P("mp", "hidden"), P("mp", "hidden"), P("hidden", "mp")),
        check_vma=False,
    )
```

```python
import functools

import jax
import jax.numpy as jnp
from jax import lax
from jax.experimental import pallas as pl
from jax.experimental.pallas import tpu as pltpu
from jax.sharding import PartitionSpec as P

MESH = pl.DeviceIdType.MESH
F32, BF16 = jnp.float32, jnp.bfloat16

NX, NY, NZ = 4, 4, 8
PIECE = 48
SHARD = 24
DM = 2304
HALF = DM // 2
FD = 384
CHUNKS = 4
PER = 4
ROWS = PIECE * PER
BLK = ROWS // NZ

XR, XL, YU, YD = (1, 0), (-1, 0), (0, 1), (0, -1)

GATHER = (
    ((1, 0), (1, 0)),
    ((-1, 0), (-1, 0)),
    ((0, 1), (0, 1)),
    ((0, -1), (0, -1)),
    ((2, 0), (1, 0)),
    ((-1, -1), (-1, 0)),
    ((0, 2), (0, 1)),
    ((1, -1), (0, -1)),
    ((1, 1), (1, 0)),
    ((2, -1), (-1, 0)),
    ((-1, 1), (0, 1)),
    ((-1, 2), (0, -1)),
    ((1, 2), (1, 0)),
    ((2, 1), (-1, 0)),
    ((2, 2), (0, -1)),
)
REDUCE = {
    (1, 0): (1, 0),
    (-1, 0): (-1, 0),
    (0, 1): (0, 1),
    (0, -1): (0, -1),
    (1, 1): (1, 1),
    (-1, 1): (-1, 1),
    (1, -1): (1, -1),
    (-1, -1): (-1, -1),
    (2, 0): (1, 0),
    (0, 2): (0, 1),
    (2, 1): (-1, 0),
    (2, -1): (1, 0),
    (1, 2): (0, -1),
    (-1, 2): (0, 1),
    (2, 2): (-1, -1),
}
CHUNK_PIECES = (
    ((0, 0), (1, 0), (-1, 0), (0, 1)),
    ((2, 0), (-1, -1), (0, 2), (1, -1)),
    ((2, 1), (2, 2), (1, 2), (2, -1)),
    ((0, -1), (1, 1), (-1, 1), (-1, 2)),
)
RING = {1: 1, 2: 1, 3: 1, 4: 1, -1: -1, -2: -1, -3: -1}
SHORT = {1: 1, 2: 2, 3: 1, 4: 2, -1: -1, -2: -1, -3: -2}
SUM_TREE = (RING, RING, RING, RING)
SPREAD_TREE = (RING, RING, RING, RING)
ORDER = (
    ("Y",), ("G", 1, 0), ("G", 3, 0), ("G", 2, 0), ("G", 12, 0),
    ("G", 1, 1), ("G", 3, 1), ("G", 2, 1), ("G", 12, 1), ("F", 0, 0),
    ("G", 7, 0), ("G", 4, 0), ("G", 6, 0), ("G", 5, 0), ("F", 0, 3),
    ("R", 0, -3), ("R", 0, 4), ("X", 0), ("G", 14, 0), ("G", 7, 1),
    ("G", 13, 0), ("G", 5, 1), ("G", 4, 1), ("G", 6, 1), ("R", 0, -2),
    ("G", 15, 0), ("G", 11, 0), ("R", 0, 3), ("F", 1, 0), ("G", 13, 1),
    ("G", 14, 1), ("F", 1, 3), ("G", 8, 0), ("G", 15, 1), ("R", 1, 4),
    ("R", 1, -3), ("R", 0, -1), ("X", 1), ("G", 10, 0), ("G", 11, 1),
    ("R", 0, 2), ("G", 9, 0), ("F", 3, 0), ("G", 10, 1), ("F", 3, 3),
    ("G", 8, 1), ("R", 1, -2), ("R", 1, 3), ("R", 3, -3), ("R", 3, 4),
    ("X", 3), ("R", 0, 1), ("G", 9, 1), ("F", 2, 0), ("R", 1, -1),
    ("R", 1, 2), ("F", 2, 3), ("R", 2, 4), ("R", 3, -2), ("R", 2, -3),
    ("A", 0), ("R", 3, 3), ("X", 2), ("R", 1, 1), ("R", 2, 3),
    ("R", 2, -2), ("R", 3, -1), ("Z", 0, -1), ("Z", 0, 1), ("R", 3, 2),
    ("R", 2, 2), ("A", 1), ("R", 2, -1), ("Z", 0, 2), ("Z", 0, -2),
    ("R", 2, 1), ("R", 3, 1), ("Z", 1, -1), ("Z", 1, 1), ("Z", 0, 3),
    ("A", 2), ("Z", 0, -3), ("Z", 1, -2), ("A", 3), ("Z", 0, 4),
    ("C", 0), ("Z", 1, 2), ("S", 0), ("W", 0, 0), ("Z", 2, 1),
    ("Z", 2, -1), ("W", 0, 1), ("W", 0, 2), ("Z", 1, -3), ("Z", 3, 1),
    ("O", 0), ("Z", 3, -1), ("Z", 1, 3), ("T", 2), ("W", 0, 3),
    ("W", 0, 4), ("Z", 2, 2), ("Z", 2, -2), ("W", 0, 5), ("Z", 3, 2),
    ("Z", 3, -2), ("Z", 1, 4), ("C", 1), ("S", 1), ("Z", 2, 3),
    ("Z", 2, -3), ("W", 1, 0), ("W", 1, 1), ("Z", 3, 3), ("W", 1, 2),
    ("O", 1), ("Z", 3, -3), ("T", 4), ("T", 6), ("W", 1, 3),
    ("Z", 2, 4), ("C", 2), ("S", 2), ("Z", 3, 4), ("C", 3),
    ("S", 3), ("W", 1, 4), ("O", 2), ("T", 9), ("T", 10),
    ("T", 8), ("T", 3), ("T", 11), ("T", 1), ("O", 3),
    ("T", 12), ("T", 15), ("T", 13), ("W", 1, 5), ("W", 2, 0),
    ("W", 2, 1), ("W", 2, 2), ("W", 2, 3), ("W", 2, 4), ("W", 2, 5),
    ("W", 3, 0), ("W", 3, 1), ("W", 3, 2), ("T", 5), ("T", 14),
    ("W", 3, 3), ("W", 3, 4), ("W", 3, 5), ("T", 7), ("E",),
)
SLOT = {p: i for i, p in enumerate(p for chunk in CHUNK_PIECES for p in chunk)}
OWN = SLOT[0, 0]


def less(p, d):
    return tuple((a - b + 1) % 4 - 1 for a, b in zip(p, d))


SOURCE = {p: less(p, d) for p, d in GATHER}
COMES = dict(GATHER)
PARENT = {p: less(p, d) for p, d in REDUCE.items()}
CHILDREN = {p: [q for q in REDUCE if PARENT[q] == p] for p in SLOT}
PIECES = {s: p for p, s in SLOT.items()}
OFFSETS = tuple(RING)
NT = (((1,), (1,)), ((), ()))
W_ORDER = [step[1] for step in ORDER if step[0] == "W" and step[2] == 0]


def dot(a, b, dims=(((1,), (0,)), ((), ()))):
    return lax.dot_general(a, b, dims, preferred_element_type=F32)


def kernel(
    x_hbm, wg_hbm, wu_hbm, wd_hbm, c_hbm,
    gi_out, gg_out, gu_out, gd_out,
    own, stage, xc, xt, wcat, wt, wd, part, rs_s, rs_r, agb, act, ht,
    gi_own, gi_s, gi_r, tr_s, tr_r, fin, acc_gu, acc_d,
    load_sem, stage_sem, ag_ss, ag_rs, sib_ss, sib_rs, rs_ss, rs_rs, za_ss, za_rs,
    gx_ss, gx_rs, tr_ss, tr_rs, fin_sem,
):
    z = lax.axis_index("mp")
    h = lax.axis_index("hidden")
    c = lax.rem(h, 2)
    chip = h // 2
    x, y = lax.rem(chip, NX), chip // NX

    def at(d):
        nx, ny = lax.rem(x + d[0] + NX, NX), lax.rem(y + d[1] + NY, NY)
        return {"hidden": (ny * NX + nx) * 2 + c}

    sibling = {"hidden": h + 1 - 2 * c}

    def zat(o):
        return lax.rem(z + o + NZ, NZ)

    def send(src, dst, ss, rs, dev):
        return pltpu.make_async_remote_copy(
            src_ref=src, dst_ref=dst, send_sem=ss, recv_sem=rs, device_id=dev, device_id_type=MESH
        )

    sent = []

    def start(copy):
        copy.start()
        sent.append(copy)

    loads = [
        pltpu.make_async_copy(x_hbm, own.at[0], load_sem.at[0]),
        pltpu.make_async_copy(c_hbm, own.at[1], load_sem.at[1]),
        pltpu.make_async_copy(wg_hbm, wcat.at[:, pl.ds(0, FD)], load_sem.at[2]),
        pltpu.make_async_copy(wu_hbm, wcat.at[:, pl.ds(FD, FD)], load_sem.at[3]),
        pltpu.make_async_copy(wd_hbm, wd, load_sem.at[4]),
    ]
    for copy in loads:
        copy.start()

    reach = sorted({d for d in COMES.values()} | {(-a, -b) for a, b in COMES.values()}
                   | set(REDUCE.values()) | {(-a, -b) for a, b in REDUCE.values()})
    reach = sorted({((a + 1) % 4 - 1, (b + 1) % 4 - 1) for a, b in reach})
    along = sorted({s * d for tree in SUM_TREE + SPREAD_TREE for d in tree.values() for s in (1, -1)})
    greet = [at(d) for d in reach] + [{"mp": zat(d)} for d in along] + [sibling]
    barrier = pltpu.get_barrier_semaphore()
    for dev in greet:
        pl.semaphore_signal(barrier, inc=1, device_id=dev, device_id_type=MESH)
    pl.semaphore_wait(barrier, len(greet))

    loads[0].wait()
    loads[1].wait()
    swap = send(own.at[1 - c], stage, stage_sem.at[0], stage_sem.at[1], sibling)
    start(swap)
    swap.wait_recv()
    mine, other = own[c].astype(F32), stage[...].astype(F32)
    first = c == 0
    xc[c, OWN] = jnp.concatenate(
        [jnp.where(first, mine, other), jnp.where(first, other, mine)], axis=0
    ).astype(BF16)

    def share(a, s, half):
        part_of = xc.at[a, s, :, pl.ds(half * HALF, HALF)]
        return send(part_of, part_of, sib_ss.at[s, half], sib_rs.at[s, half], sibling)

    def hop(p, half):
        s, d, cols = SLOT[p], COMES[p], pl.ds(half * HALF, HALF)
        return send(
            xc.at[c, SLOT[SOURCE[p]], :, cols], xc.at[c, s, :, cols],
            ag_ss.at[s, half], ag_rs.at[s, half], at((-d[0], -d[1])),
        )

    def forward(q, half):
        for p, _ in GATHER:
            if SOURCE[p] == q:
                start(hop(p, half))

    def gather(s, half):
        hop(PIECES[s], half).wait_recv()
        forward(PIECES[s], half)
        start(share(c, s, half))

    for half in (0, 1):
        forward((0, 0), half)
    for half in (0, 1):
        start(share(c, OWN, half))

    def flip_weights():
        for copy in loads[2:]:
            copy.wait()

        def tile(n, _):
            cols = pl.ds(pl.multiple_of(n * 256, 256), 256)
            wt[:, cols] = wcat[cols, :].T
            return 0

        lax.fori_loop(0, DM // 256, tile, 0)

    def flip_inputs(k):
        def tile(n, _):
            cols = pl.ds(pl.multiple_of(n * 256, 256), 256)
            xt[k, cols, pl.ds(0, ROWS)] = xc[0, pl.ds(PER * k, PER), :, cols].reshape(ROWS, 256).T
            return 0

        lax.fori_loop(0, DM // 256, tile, 0)

    def rows_of(a, k):
        return xc[a, pl.ds(PER * k, PER)].reshape(ROWS, DM)

    def product(k, n):
        if n == 0:
            for i in range(PER * k, PER * k + PER):
                for half in (0, 1):
                    share(1 - c, i, half).wait_recv()
            part[k, :, :, pl.ds(0, 2 * FD)] = dot(rows_of(0, k), wcat[...]).reshape(NZ, BLK, 2 * FD)
        else:
            part[k, :, :, pl.ds(2 * FD, FD)] = dot(rows_of(1, k), wd[...], NT).reshape(NZ, BLK, FD)

    def sign(k):
        return 1 if k % 2 == 0 else -1

    def sum_copy(k, o):
        m = OFFSETS.index(o)
        dev = {"mp": zat(sign(k) * SUM_TREE[k][o])}
        return send(rs_s.at[k, m], rs_r.at[k, m], rs_ss.at[k, m], rs_rs.at[k, m], dev)

    def sum_at(k, o):
        value = part[k, zat(sign(k) * o)]
        for q, d in SUM_TREE[k].items():
            if q - d == o:
                sum_copy(k, q).wait_recv()
                value = value + rs_r[k, OFFSETS.index(q)].astype(F32)
        return value

    def reduce(k, o):
        rs_s[k, OFFSETS.index(o)] = sum_at(k, o).astype(BF16)
        start(sum_copy(k, o))

    def spread_copy(k, o):
        m, d = OFFSETS.index(o), SPREAD_TREE[k][o]
        block = agb.at[k, zat(-sign(k) * (o - d))]
        return send(block, block, za_ss.at[k, m], za_rs.at[k, m], {"mp": zat(sign(k) * d)})

    def spread_wait(k, o):
        m, d = OFFSETS.index(o), SPREAD_TREE[k][o]
        block = agb.at[k, zat(-sign(k) * o)]
        send(block, block, za_ss.at[k, m], za_rs.at[k, m], {"mp": zat(sign(k) * d)}).wait_recv()

    def spread_on(k, q):
        for o, d in SPREAD_TREE[k].items():
            if o - d == q:
                start(spread_copy(k, o))

    def spread(k, o):
        spread_wait(k, o)
        spread_on(k, o)

    def activate(k):
        total = sum_at(k, 0)
        gate, up, dhid = total[:, :FD], total[:, FD : 2 * FD], total[:, 2 * FD :]
        sig = jax.nn.sigmoid(gate)
        agb[k, z] = jnp.concatenate(
            [
                gate * sig * up,
                dhid * up * sig * (1.0 + gate * (1.0 - sig)),
                dhid * gate * sig,
            ],
            axis=1,
        ).astype(BF16)
        spread_on(k, 0)

    def collect(k):
        act[k] = jnp.concatenate([agb[k, j].astype(F32) for j in range(NZ)], axis=0).astype(BF16)
        ht[k, :, pl.ds(0, ROWS)] = act[k, :, pl.ds(0, FD)].T

    def gi_swap(k):
        s = pl.ds(PER * k, PER)
        return send(gi_s.at[s], gi_r.at[s], gx_ss.at[k], gx_rs.at[k], sibling)

    def input_grad(k, half, dst):
        cols = pl.ds(pl.multiple_of(half * HALF, 128), HALF)
        value = dot(act[k, :, pl.ds(FD, 2 * FD)], wt[:, cols])
        dst[pl.ds(PER * k, PER)] = value.reshape(PER, PIECE, HALF).astype(dst.dtype)

    def their_half(k):
        input_grad(k, 1 - c, gi_s)
        start(gi_swap(k))

    def our_half(k):
        input_grad(k, c, gi_own)
        gi_swap(k).wait_recv()

    def tr_copy(p):
        s = SLOT[p]
        return send(tr_s.at[s], tr_r.at[s], tr_ss.at[s], tr_rs.at[s], at(REDUCE[p]))

    def tree_sum(p):
        s = SLOT[p]
        value = gi_own[s] + gi_r[s].astype(F32)
        for q in CHILDREN[p]:
            tr_copy(q).wait_recv()
            value = value + tr_r[SLOT[q]].astype(F32)
        return value

    def tree(s):
        tr_s[s] = tree_sum(PIECES[s]).astype(BF16)
        start(tr_copy(PIECES[s]))

    def weight_grads(k, i):
        last = k == W_ORDER[-1]
        slots = pl.ds(PER * k, PER)

        cols = pl.ds(DM // 3 * (i % 3), DM // 3)
        if i < 3:
            value = dot(xt[k, cols, pl.ds(0, ROWS)], act[k, :, pl.ds(FD, 2 * FD)])
            if k != W_ORDER[0]:
                value = value + acc_gu[cols, :]
            if last:
                gg_out[cols, :] = value[:, :FD].astype(BF16)
                gu_out[cols, :] = value[:, FD:].astype(BF16)
            else:
                acc_gu[cols, :] = value
        else:
            value = dot(ht[k, :, pl.ds(0, ROWS)], xc[1, slots, :, cols].reshape(ROWS, DM // 3))
            if k != W_ORDER[0]:
                value = value + acc_d[:, cols]
            if last:
                gd_out[:, cols] = value.astype(BF16)
            else:
                acc_d[:, cols] = value

    def finish():
        gi_own[OWN] = tree_sum((0, 0))
        theirs = pl.ds(pl.multiple_of((1 - c) * SHARD, 8), SHARD)
        ours = pl.ds(pl.multiple_of(c * SHARD, 8), SHARD)
        fin[1] = gi_own[OWN, theirs, :].astype(BF16)
        copy = send(fin.at[1], fin.at[0], fin_sem.at[0], fin_sem.at[1], sibling)
        start(copy)
        gi_out[:, pl.ds(pl.multiple_of(c * HALF, 128), HALF)] = gi_own[OWN, ours, :].astype(BF16)
        copy.wait_recv()
        gi_out[:, pl.ds(pl.multiple_of((1 - c) * HALF, 128), HALF)] = fin[0]

    steps = {
        "G": gather, "F": product, "R": reduce, "A": activate, "Z": spread, "C": collect,
        "S": their_half, "O": our_half, "T": tree, "W": weight_grads, "E": finish, "X": flip_inputs, "Y": flip_weights,
    }
    for step, *numbers in ORDER:
        steps[step](*numbers)
    for copy in sent:
        copy.wait_send()


def store(*refs):
    n = len(refs) // 2
    copies = [pltpu.make_async_copy(refs[i], refs[n + i], refs[-1].at[i]) for i in range(n)]
    for copy in copies:
        copy.start()
    for copy in copies:
        copy.wait()


def shards(inputs, gate_weight, up_weight, down_weight, cotangent):
    dma = pltpu.SemaphoreType.DMA
    any_spec = pl.BlockSpec(memory_space=pl.ANY)
    slots, offsets = CHUNKS * PER, len(OFFSETS)
    shapes = ((SHARD, DM), (DM, FD), (DM, FD), (FD, DM))
    results = pl.pallas_call(
        kernel,
        out_shape=tuple(pltpu.VMEM(shape, BF16) for shape in shapes),
        in_specs=[any_spec] * 5,
        out_specs=(pl.BlockSpec(memory_space=pltpu.VMEM),) * 4,
        scratch_shapes=[
            pltpu.VMEM((2, SHARD, DM), BF16),
            pltpu.VMEM((SHARD, DM), BF16),
            pltpu.VMEM((2, slots, PIECE, DM), BF16),
            pltpu.VMEM((CHUNKS, DM, 256), BF16),
            pltpu.VMEM((DM, 2 * FD), BF16),
            pltpu.VMEM((2 * FD, DM), BF16),
            pltpu.VMEM((FD, DM), BF16),
            pltpu.VMEM((CHUNKS, NZ, BLK, 3 * FD), F32),
            pltpu.VMEM((CHUNKS, offsets, BLK, 3 * FD), BF16),
            pltpu.VMEM((CHUNKS, offsets, BLK, 3 * FD), BF16),
            pltpu.VMEM((CHUNKS, NZ, BLK, 3 * FD), BF16),
            pltpu.VMEM((CHUNKS, ROWS, 3 * FD), BF16),
            pltpu.VMEM((CHUNKS, FD, 256), BF16),
            pltpu.VMEM((slots, PIECE, HALF), F32),
            pltpu.VMEM((slots, PIECE, HALF), BF16),
            pltpu.VMEM((slots, PIECE, HALF), BF16),
            pltpu.VMEM((slots, PIECE, HALF), BF16),
            pltpu.VMEM((slots, PIECE, HALF), BF16),
            pltpu.VMEM((2, SHARD, HALF), BF16),
            pltpu.VMEM((DM, 2 * FD), F32),
            pltpu.VMEM((FD, DM), F32),
            dma((5,)),
            dma((2,)),
            dma((slots, 2)), dma((slots, 2)),
            dma((slots, 2)), dma((slots, 2)),
            dma((CHUNKS, offsets)), dma((CHUNKS, offsets)),
            dma((CHUNKS, offsets)), dma((CHUNKS, offsets)),
            dma((CHUNKS,)), dma((CHUNKS,)),
            dma((slots,)), dma((slots,)),
            dma((2,)),
        ],
        compiler_params=pltpu.CompilerParams(
            collective_id=0, has_side_effects=True, vmem_limit_bytes=57 * 1024 * 1024
        ),
    )(inputs, gate_weight, up_weight, down_weight, cotangent)
    return pl.pallas_call(
        store,
        out_shape=tuple(jax.ShapeDtypeStruct(shape, BF16) for shape in shapes),
        in_specs=[pl.BlockSpec(memory_space=pltpu.VMEM)] * 4,
        out_specs=(any_spec,) * 4,
        scratch_shapes=[dma((4,))],
        compiler_params=pltpu.CompilerParams(vmem_limit_bytes=1024 * 1024),
    )(*(pltpu.with_memory_space_constraint(a, pltpu.VMEM) for a in results))


def solution(mesh):
    placed = (
        P("hidden", "mp"),
        P("mp", "hidden"),
        P("mp", "hidden"),
        P("hidden", "mp"),
        P("hidden", "mp"),
    )
    return jax.shard_map(
        shards,
        mesh=mesh,
        in_specs=placed,
        out_specs=(P("hidden", "mp"), P("mp", "hidden"), P("mp", "hidden"), P("hidden", "mp")),
        check_vma=False,
    )
```

```python
import functools

import jax
import jax.numpy as jnp
from jax import lax
from jax.experimental import pallas as pl
from jax.experimental.pallas import tpu as pltpu
from jax.sharding import PartitionSpec as P

MESH = pl.DeviceIdType.MESH
F32, BF16 = jnp.float32, jnp.bfloat16

NX, NY, NZ = 4, 4, 8
PIECE = 48
SHARD = 24
DM = 2304
HALF = DM // 2
FD = 384
CHUNKS = 4
PER = 4
ROWS = PIECE * PER
BLK = ROWS // NZ

XR, XL, YU, YD = (1, 0), (-1, 0), (0, 1), (0, -1)

GATHER = (
    ((1, 0), (1, 0)),
    ((-1, 0), (-1, 0)),
    ((0, 1), (0, 1)),
    ((0, -1), (0, -1)),
    ((2, 0), (1, 0)),
    ((-1, -1), (-1, 0)),
    ((0, 2), (0, 1)),
    ((1, -1), (0, -1)),
    ((1, 1), (1, 0)),
    ((2, -1), (-1, 0)),
    ((-1, 1), (0, 1)),
    ((-1, 2), (0, -1)),
    ((1, 2), (1, 0)),
    ((2, 1), (-1, 0)),
    ((2, 2), (0, -1)),
)
REDUCE = {
    (1, 0): (1, 0),
    (-1, 0): (-1, 0),
    (0, 1): (0, 1),
    (0, -1): (0, -1),
    (1, 1): (1, 1),
    (-1, 1): (-1, 1),
    (1, -1): (1, -1),
    (-1, -1): (-1, -1),
    (2, 0): (1, 0),
    (0, 2): (0, 1),
    (2, 1): (-1, 0),
    (2, -1): (1, 0),
    (1, 2): (0, -1),
    (-1, 2): (0, 1),
    (2, 2): (-1, -1),
}
CHUNK_PIECES = (
    ((0, 0), (1, 0), (-1, 0), (0, 1)),
    ((2, 0), (-1, -1), (0, 2), (1, -1)),
    ((2, 1), (2, 2), (1, 2), (2, -1)),
    ((0, -1), (1, 1), (-1, 1), (-1, 2)),
)
SUM_TREE = (
    {1: 1, 2: 1, 3: 1, 4: 1, -1: -1, -2: -1, -3: -1},
    {1: 1, 2: 1, 3: 1, 4: 1, -1: -1, -2: -1, -3: -1},
    {1: 1, 2: 1, 3: 1, 4: 1, -1: -1, -2: -1, -3: -1},
    {1: 1, 2: 1, 3: 1, 4: 1, -1: -1, -2: -1, -3: -1},
    {1: 1, 2: 1, 3: 1, 4: 1, -1: -1, -2: -1, -3: -1},
    {1: 1, 2: 1, 3: 1, 4: 1, -1: -1, -2: -1, -3: -1},
    {1: 1, 2: 1, 3: 1, 4: 1, -1: -1, -2: -1, -3: -1},
    {1: 1, 2: 1, 3: 1, 4: 1, -1: -1, -2: -1, -3: -1},
)
SUM_SIGN = (1, 1, -1, -1, 1, 1, -1, -1)
SPREAD_TREE = (
    {1: 1, 2: 1, 3: 1, 4: 1, -1: -1, -2: -1, -3: -1},
    {1: 1, 2: 1, 3: 1, 4: 1, -1: -1, -2: -1, -3: -1},
    {1: 1, 2: 1, 3: 1, 4: 1, -1: -1, -2: -1, -3: -1},
    {1: 1, 2: 1, 3: 1, 4: 1, -1: -1, -2: -1, -3: -1},
)
SPREAD_SIGN = (1, -1, 1, -1)
ORDER = (
    ("Y",), ("I",), ("G", 1, 0), ("G", 3, 0), ("G", 2, 0), ("G", 12, 0),
    ("F", 0, 0), ("R", 0, 4), ("R", 0, -3), ("G", 1, 1), ("G", 3, 1), ("G", 12, 1),
    ("G", 2, 1), ("X", 0), ("F", 0, 3), ("R", 1, 4), ("R", 1, -3), ("G", 4, 0),
    ("G", 6, 0), ("G", 7, 0), ("G", 5, 0), ("R", 0, 3), ("R", 0, -2), ("F", 1, 0),
    ("X", 1), ("R", 1, -2), ("G", 5, 1), ("G", 13, 0), ("G", 7, 1), ("R", 1, 3),
    ("R", 2, 4), ("R", 2, -3), ("G", 14, 0), ("R", 0, 2), ("R", 0, -1), ("G", 4, 1),
    ("G", 6, 1), ("G", 11, 0), ("G", 15, 0), ("F", 1, 3), ("R", 1, -1), ("R", 1, 2),
    ("R", 3, 4), ("R", 3, -3), ("F", 3, 0), ("G", 13, 1), ("G", 14, 1), ("R", 6, 4),
    ("R", 2, -2), ("R", 6, -3), ("R", 2, 3), ("R", 0, 1), ("X", 3), ("G", 11, 1),
    ("G", 15, 1), ("G", 10, 0), ("F", 3, 3), ("R", 1, 1), ("R", 7, 4), ("R", 3, 3),
    ("R", 7, -3), ("R", 3, -2), ("G", 8, 0), ("G", 9, 0), ("R", 6, 3), ("R", 2, -1),
    ("G", 10, 1), ("R", 2, 2), ("R", 6, -2), ("F", 2, 0), ("R", 4, -3), ("R", 4, 4),
    ("X", 2), ("G", 8, 1), ("A", 0), ("R", 7, 3), ("G", 9, 1), ("R", 7, -2),
    ("R", 3, 2), ("R", 3, -1), ("R", 6, 2), ("F", 2, 3), ("R", 5, 4), ("R", 5, -3),
    ("R", 2, 1), ("R", 6, -1), ("R", 4, -2), ("R", 4, 3), ("Z", 0, 1), ("Z", 0, -1),
    ("R", 7, 2), ("R", 7, -1), ("R", 3, 1), ("R", 5, 3), ("R", 6, 1), ("R", 5, -2),
    ("R", 4, 2), ("R", 4, -1), ("Z", 0, -2), ("Z", 0, 2), ("R", 5, 2), ("R", 7, 1),
    ("A", 1), ("R", 4, 1), ("R", 5, -1), ("Z", 0, -3), ("R", 5, 1), ("Z", 0, 3),
    ("A", 3), ("Z", 1, 1), ("Z", 1, -1), ("A", 2), ("Z", 0, 4), ("C", 0),
    ("S", 0), ("Z", 3, 1), ("Z", 3, -1), ("Z", 1, 2), ("O", 0), ("Z", 1, -2),
    ("T", 2), ("Z", 2, -1), ("Z", 2, 1), ("Z", 3, 2), ("Z", 3, -2), ("Z", 1, 3),
    ("Z", 1, -3), ("Z", 2, -2), ("Z", 2, 2), ("Z", 3, 3), ("Z", 3, -3), ("Z", 1, 4),
    ("C", 1), ("S", 1), ("W", 1, 4), ("W", 1, 3), ("W", 1, 5), ("W", 0, 5),
    ("Z", 2, 3), ("Z", 2, -3), ("O", 1), ("T", 6), ("T", 4), ("Z", 3, 4),
    ("C", 3), ("S", 3), ("W", 0, 4), ("W", 1, 0), ("W", 0, 0), ("W", 1, 1),
    ("O", 3), ("T", 12), ("T", 15), ("T", 13), ("Z", 2, 4), ("C", 2),
    ("S", 2), ("W", 2, 4), ("W", 3, 4), ("W", 2, 0), ("W", 3, 0), ("O", 2),
    ("T", 10), ("T", 3), ("T", 9), ("T", 8), ("T", 11), ("W", 2, 5),
    ("W", 3, 5), ("T", 1), ("W", 0, 3), ("W", 2, 3), ("W", 3, 3), ("W", 1, 2),
    ("W", 0, 2), ("W", 2, 2), ("W", 3, 2), ("W", 0, 1), ("W", 2, 1), ("W", 3, 1),
    ("T", 7), ("T", 14), ("T", 5), ("E",),
)
SLOT = {p: i for i, p in enumerate(p for chunk in CHUNK_PIECES for p in chunk)}
OWN = SLOT[0, 0]


def less(p, d):
    return tuple((a - b + 1) % 4 - 1 for a, b in zip(p, d))


SOURCE = {p: less(p, d) for p, d in GATHER}
COMES = dict(GATHER)
PARENT = {p: less(p, d) for p, d in REDUCE.items()}
CHILDREN = {p: [q for q in REDUCE if PARENT[q] == p] for p in SLOT}
PIECES = {s: p for p, s in SLOT.items()}
OFFSETS = (1, 2, 3, 4, -1, -2, -3)
NT = (((1,), (1,)), ((), ()))
W_ORDER = [step[1] for step in ORDER if step[0] == "W" and step[2] == 0]


def dot(a, b, dims=(((1,), (0,)), ((), ()))):
    return lax.dot_general(a, b, dims, preferred_element_type=F32)


def kernel(
    x_hbm, wg_hbm, wu_hbm, wd_hbm, c_hbm,
    gi_out, gg_out, gu_out, gd_out,
    own, stage, xc, xt, wcat, wt, wd, part, gu_s, gu_r, dh_s, dh_r, agb, act, ht,
    gi_own, gi_s, gi_r, tr_s, tr_r, fin, acc_gu, acc_d,
    load_sem, stage_sem, ag_ss, ag_rs, sib_ss, sib_rs, rs_ss, rs_rs, za_ss, za_rs,
    gx_ss, gx_rs, tr_ss, tr_rs, fin_sem,
):
    z = lax.axis_index("mp")
    h = lax.axis_index("hidden")
    c = lax.rem(h, 2)
    chip = h // 2
    x, y = lax.rem(chip, NX), chip // NX

    def at(d):
        nx, ny = lax.rem(x + d[0] + NX, NX), lax.rem(y + d[1] + NY, NY)
        return {"hidden": (ny * NX + nx) * 2 + c}

    sibling = {"hidden": h + 1 - 2 * c}

    def zat(o):
        return lax.rem(z + o + NZ, NZ)

    def send(src, dst, ss, rs, dev):
        return pltpu.make_async_remote_copy(
            src_ref=src, dst_ref=dst, send_sem=ss, recv_sem=rs, device_id=dev, device_id_type=MESH
        )

    sent = []

    def start(copy):
        copy.start()
        sent.append(copy)

    loads = [
        pltpu.make_async_copy(x_hbm, own.at[0], load_sem.at[0]),
        pltpu.make_async_copy(c_hbm, own.at[1], load_sem.at[1]),
        pltpu.make_async_copy(wg_hbm, wcat.at[:, pl.ds(0, FD)], load_sem.at[2]),
        pltpu.make_async_copy(wu_hbm, wcat.at[:, pl.ds(FD, FD)], load_sem.at[3]),
        pltpu.make_async_copy(wd_hbm, wd, load_sem.at[4]),
    ]
    for copy in loads:
        copy.start()

    reach = sorted({d for d in COMES.values()} | {(-a, -b) for a, b in COMES.values()}
                   | set(REDUCE.values()) | {(-a, -b) for a, b in REDUCE.values()})
    reach = sorted({((a + 1) % 4 - 1, (b + 1) % 4 - 1) for a, b in reach})
    along = sorted({s * d for tree in SUM_TREE + SPREAD_TREE for d in tree.values() for s in (1, -1)})
    greet = [at(d) for d in reach] + [{"mp": zat(d)} for d in along] + [sibling]
    barrier = pltpu.get_barrier_semaphore()
    for dev in greet:
        pl.semaphore_signal(barrier, inc=1, device_id=dev, device_id_type=MESH)
    pl.semaphore_wait(barrier, len(greet))

    ours = pl.ds(pl.multiple_of(c * HALF, 128), HALF)
    theirs = pl.ds(pl.multiple_of((1 - c) * HALF, 128), HALF)

    def swap(a):
        return send(own.at[a, :, theirs], stage.at[a], stage_sem.at[0, a], stage_sem.at[1, a], sibling)

    for a in (0, 1):
        loads[a].wait()
        start(swap(a))

    def share(a, s, cols):
        block = xc.at[a, s, :, cols]
        return send(block, block, sib_ss.at[s, a], sib_rs.at[s, a], sibling)

    def hop(p, a):
        s, d = SLOT[p], COMES[p]
        return send(
            xc.at[a, SLOT[SOURCE[p]], :, ours], xc.at[a, s, :, ours],
            ag_ss.at[s, a], ag_rs.at[s, a], at((-d[0], -d[1])),
        )

    def forward(q, a):
        for p, _ in GATHER:
            if SOURCE[p] == q:
                start(hop(p, a))

    def gather(s, a):
        hop(PIECES[s], a).wait_recv()
        forward(PIECES[s], a)
        start(share(a, s, ours))

    def begin(a):
        swap(a).wait_recv()
        mine, other = own[a, :, ours].astype(F32), stage[a].astype(F32)
        first = c == 0
        xc[a, OWN, :, ours] = jnp.concatenate(
            [jnp.where(first, mine, other), jnp.where(first, other, mine)], axis=0
        ).astype(BF16)
        forward((0, 0), a)
        start(share(a, OWN, ours))

    begin(0)

    def flip_weights():
        for copy in loads[2:]:
            copy.wait()

        def tile(n, _):
            cols = pl.ds(pl.multiple_of(n * 256, 256), 256)
            wt[:, cols] = wcat[cols, :].T
            return 0

        lax.fori_loop(0, DM // 256, tile, 0)

    def flip_inputs(k):
        def tile(n, _):
            cols = pl.ds(pl.multiple_of(n * 256, 256), 256)
            xt[k, cols, pl.ds(0, ROWS)] = xc[0, pl.ds(PER * k, PER), :, cols].reshape(ROWS, 256).T
            return 0

        lax.fori_loop(0, DM // 256, tile, 0)

    def rows_of(a, k):
        return xc[a, pl.ds(PER * k, PER)].reshape(ROWS, DM)

    def product(k, n):
        a = 0 if n == 0 else 1
        for i in range(PER * k, PER * k + PER):
            share(a, i, theirs).wait_recv()
        if n == 0:
            part[k, :, :, pl.ds(0, 2 * FD)] = dot(rows_of(0, k), wcat[...]).reshape(NZ, BLK, 2 * FD)
        else:
            part[k, :, :, pl.ds(2 * FD, FD)] = dot(rows_of(1, k), wd[...], NT).reshape(NZ, BLK, FD)

    def sum_copy(u, o):
        k, j, m = u // 2, u % 2, OFFSETS.index(o)
        src, dst = (dh_s, dh_r) if j else (gu_s, gu_r)
        dev = {"mp": zat(SUM_SIGN[u] * SUM_TREE[u][o])}
        return send(src.at[k, m], dst.at[k, m], rs_ss.at[u, m], rs_rs.at[u, m], dev)

    def sum_at(u, o):
        k, j = u // 2, u % 2
        cols, landed = (pl.ds(2 * FD, FD), dh_r) if j else (pl.ds(0, 2 * FD), gu_r)
        value = part[k, zat(SUM_SIGN[u] * o), :, cols]
        for q, d in SUM_TREE[u].items():
            if q - d == o:
                sum_copy(u, q).wait_recv()
                value = value + landed[k, OFFSETS.index(q)].astype(F32)
        return value

    def reduce(u, o):
        (dh_s if u % 2 else gu_s)[u // 2, OFFSETS.index(o)] = sum_at(u, o).astype(BF16)
        start(sum_copy(u, o))

    def spread_copy(k, o):
        m, d = OFFSETS.index(o), SPREAD_TREE[k][o]
        block = agb.at[k, zat(SPREAD_SIGN[k] * (o - d))]
        return send(block, block, za_ss.at[k, m], za_rs.at[k, m], {"mp": zat(-SPREAD_SIGN[k] * d)})

    def spread_wait(k, o):
        m, d = OFFSETS.index(o), SPREAD_TREE[k][o]
        block = agb.at[k, zat(SPREAD_SIGN[k] * o)]
        send(block, block, za_ss.at[k, m], za_rs.at[k, m], {"mp": zat(-SPREAD_SIGN[k] * d)}).wait_recv()

    def spread_on(k, q):
        for o, d in SPREAD_TREE[k].items():
            if o - d == q:
                start(spread_copy(k, o))

    def spread(k, o):
        spread_wait(k, o)
        spread_on(k, o)

    def activate(k):
        both, dhid = sum_at(2 * k, 0), sum_at(2 * k + 1, 0)
        gate, up = both[:, :FD], both[:, FD:]
        sig = jax.nn.sigmoid(gate)
        agb[k, z] = jnp.concatenate(
            [
                gate * sig * up,
                dhid * up * sig * (1.0 + gate * (1.0 - sig)),
                dhid * gate * sig,
            ],
            axis=1,
        ).astype(BF16)
        spread_on(k, 0)

    def collect(k):
        act[k] = jnp.concatenate([agb[k, j].astype(F32) for j in range(NZ)], axis=0).astype(BF16)
        ht[k, :, pl.ds(0, ROWS)] = act[k, :, pl.ds(0, FD)].T

    def gi_swap(k):
        s = pl.ds(PER * k, PER)
        return send(gi_s.at[s], gi_r.at[s], gx_ss.at[k], gx_rs.at[k], sibling)

    def input_grad(k, half, dst):
        cols = pl.ds(pl.multiple_of(half * HALF, 128), HALF)
        value = dot(act[k, :, pl.ds(FD, 2 * FD)], wt[:, cols])
        dst[pl.ds(PER * k, PER)] = value.reshape(PER, PIECE, HALF).astype(dst.dtype)

    def their_half(k):
        input_grad(k, 1 - c, gi_s)
        start(gi_swap(k))

    def our_half(k):
        input_grad(k, c, gi_own)
        gi_swap(k).wait_recv()

    def tr_copy(p):
        s = SLOT[p]
        return send(tr_s.at[s], tr_r.at[s], tr_ss.at[s], tr_rs.at[s], at(REDUCE[p]))

    def tree_sum(p):
        s = SLOT[p]
        value = gi_own[s] + gi_r[s].astype(F32)
        for q in CHILDREN[p]:
            tr_copy(q).wait_recv()
            value = value + tr_r[SLOT[q]].astype(F32)
        return value

    def tree(s):
        tr_s[s] = tree_sum(PIECES[s]).astype(BF16)
        start(tr_copy(PIECES[s]))

    def weight_grads(k, i):
        last = k == W_ORDER[-1]
        slots = pl.ds(PER * k, PER)

        cols = pl.ds(DM // 3 * (i % 3), DM // 3)
        if i < 3:
            value = dot(xt[k, cols, pl.ds(0, ROWS)], act[k, :, pl.ds(FD, 2 * FD)])
            if k != W_ORDER[0]:
                value = value + acc_gu[cols, :]
            if last:
                gg_out[cols, :] = value[:, :FD].astype(BF16)
                gu_out[cols, :] = value[:, FD:].astype(BF16)
            else:
                acc_gu[cols, :] = value
        else:
            value = dot(ht[k, :, pl.ds(0, ROWS)], xc[1, slots, :, cols].reshape(ROWS, DM // 3))
            if k != W_ORDER[0]:
                value = value + acc_d[:, cols]
            if last:
                gd_out[:, cols] = value.astype(BF16)
            else:
                acc_d[:, cols] = value

    def finish():
        gi_own[OWN] = tree_sum((0, 0))
        sent_rows = pl.ds(pl.multiple_of((1 - c) * SHARD, 8), SHARD)
        kept_rows = pl.ds(pl.multiple_of(c * SHARD, 8), SHARD)
        fin[1] = gi_own[OWN, sent_rows, :].astype(BF16)
        copy = send(fin.at[1], fin.at[0], fin_sem.at[0], fin_sem.at[1], sibling)
        start(copy)
        gi_out[:, ours] = gi_own[OWN, kept_rows, :].astype(BF16)
        copy.wait_recv()
        gi_out[:, theirs] = fin[0]

    steps = {
        "G": gather, "F": product, "R": reduce, "A": activate, "Z": spread, "C": collect,
        "S": their_half, "O": our_half, "T": tree, "W": weight_grads, "E": finish, "X": flip_inputs, "Y": flip_weights,
        "I": lambda: begin(1),
    }
    for step, *numbers in ORDER:
        steps[step](*numbers)
    for copy in sent:
        copy.wait_send()


def store(*refs):
    n = len(refs) // 2
    copies = [pltpu.make_async_copy(refs[i], refs[n + i], refs[-1].at[i]) for i in range(n)]
    for copy in copies:
        copy.start()
    for copy in copies:
        copy.wait()


def shards(inputs, gate_weight, up_weight, down_weight, cotangent):
    dma = pltpu.SemaphoreType.DMA
    any_spec = pl.BlockSpec(memory_space=pl.ANY)
    slots, offsets = CHUNKS * PER, len(OFFSETS)
    shapes = ((SHARD, DM), (DM, FD), (DM, FD), (FD, DM))
    results = pl.pallas_call(
        kernel,
        out_shape=tuple(pltpu.VMEM(shape, BF16) for shape in shapes),
        in_specs=[any_spec] * 5,
        out_specs=(pl.BlockSpec(memory_space=pltpu.VMEM),) * 4,
        scratch_shapes=[
            pltpu.VMEM((2, SHARD, DM), BF16),
            pltpu.VMEM((2, SHARD, HALF), BF16),
            pltpu.VMEM((2, slots, PIECE, DM), BF16),
            pltpu.VMEM((CHUNKS, DM, 256), BF16),
            pltpu.VMEM((DM, 2 * FD), BF16),
            pltpu.VMEM((2 * FD, DM), BF16),
            pltpu.VMEM((FD, DM), BF16),
            pltpu.VMEM((CHUNKS, NZ, BLK, 3 * FD), F32),
            pltpu.VMEM((CHUNKS, offsets, BLK, 2 * FD), BF16),
            pltpu.VMEM((CHUNKS, offsets, BLK, 2 * FD), BF16),
            pltpu.VMEM((CHUNKS, offsets, BLK, FD), BF16),
            pltpu.VMEM((CHUNKS, offsets, BLK, FD), BF16),
            pltpu.VMEM((CHUNKS, NZ, BLK, 3 * FD), BF16),
            pltpu.VMEM((CHUNKS, ROWS, 3 * FD), BF16),
            pltpu.VMEM((CHUNKS, FD, 256), BF16),
            pltpu.VMEM((slots, PIECE, HALF), F32),
            pltpu.VMEM((slots, PIECE, HALF), BF16),
            pltpu.VMEM((slots, PIECE, HALF), BF16),
            pltpu.VMEM((slots, PIECE, HALF), BF16),
            pltpu.VMEM((slots, PIECE, HALF), BF16),
            pltpu.VMEM((2, SHARD, HALF), BF16),
            pltpu.VMEM((DM, 2 * FD), F32),
            pltpu.VMEM((FD, DM), F32),
            dma((5,)),
            dma((2, 2)),
            dma((slots, 2)), dma((slots, 2)),
            dma((slots, 2)), dma((slots, 2)),
            dma((2 * CHUNKS, offsets)), dma((2 * CHUNKS, offsets)),
            dma((CHUNKS, offsets)), dma((CHUNKS, offsets)),
            dma((CHUNKS,)), dma((CHUNKS,)),
            dma((slots,)), dma((slots,)),
            dma((2,)),
        ],
        compiler_params=pltpu.CompilerParams(
            collective_id=0, has_side_effects=True, vmem_limit_bytes=57 * 1024 * 1024
        ),
    )(inputs, gate_weight, up_weight, down_weight, cotangent)
    return pl.pallas_call(
        store,
        out_shape=tuple(jax.ShapeDtypeStruct(shape, BF16) for shape in shapes),
        in_specs=[pl.BlockSpec(memory_space=pltpu.VMEM)] * 4,
        out_specs=(any_spec,) * 4,
        scratch_shapes=[dma((4,))],
        compiler_params=pltpu.CompilerParams(vmem_limit_bytes=1024 * 1024),
    )(*(pltpu.with_memory_space_constraint(a, pltpu.VMEM) for a in results))


def solution(mesh):
    placed = (
        P("hidden", "mp"),
        P("mp", "hidden"),
        P("mp", "hidden"),
        P("hidden", "mp"),
        P("hidden", "mp"),
    )
    return jax.shard_map(
        shards,
        mesh=mesh,
        in_specs=placed,
        out_specs=(P("hidden", "mp"), P("mp", "hidden"), P("mp", "hidden"), P("hidden", "mp")),
        check_vma=False,
    )
```

```python
import functools

import jax
import jax.numpy as jnp
from jax import lax
from jax.experimental import pallas as pl
from jax.experimental.pallas import tpu as pltpu
from jax.sharding import PartitionSpec as P

MESH = pl.DeviceIdType.MESH
F32, BF16 = jnp.float32, jnp.bfloat16

NX, NY, NZ = 4, 4, 8
PIECE = 48
SHARD = 24
DM = 2304
HALF = DM // 2
FD = 384
CHUNKS = 4
PER = 4
ROWS = PIECE * PER
BLK = ROWS // NZ

XR, XL, YU, YD = (1, 0), (-1, 0), (0, 1), (0, -1)

GATHER = (
    ((1, 0), (1, 0)),
    ((-1, 0), (-1, 0)),
    ((0, 1), (0, 1)),
    ((0, -1), (0, -1)),
    ((2, 0), (1, 0)),
    ((-1, -1), (-1, 0)),
    ((0, 2), (0, 1)),
    ((1, -1), (0, -1)),
    ((1, 1), (1, 0)),
    ((2, -1), (-1, 0)),
    ((-1, 1), (0, 1)),
    ((-1, 2), (0, -1)),
    ((1, 2), (1, 0)),
    ((2, 1), (-1, 0)),
    ((2, 2), (0, -1)),
)
REDUCE = {
    (1, 0): (1, 0),
    (-1, 0): (-1, 0),
    (0, 1): (0, 1),
    (0, -1): (0, -1),
    (1, 1): (1, 1),
    (-1, 1): (-1, 1),
    (1, -1): (1, -1),
    (-1, -1): (-1, -1),
    (2, 0): (1, 0),
    (0, 2): (0, 1),
    (2, 1): (-1, 0),
    (2, -1): (1, 0),
    (1, 2): (0, -1),
    (-1, 2): (0, 1),
    (2, 2): (-1, -1),
}
CHUNK_PIECES = (
    ((0, 0), (1, 0), (-1, 0), (0, 1)),
    ((2, 0), (-1, -1), (0, 2), (1, -1)),
    ((2, 1), (2, 2), (1, 2), (2, -1)),
    ((0, -1), (1, 1), (-1, 1), (-1, 2)),
)
SUM_TREE = (
    {1: 1, 2: 1, 3: 1, 4: 1, -1: -1, -2: -1, -3: -1},
    {1: 1, 2: 1, 3: 1, 4: 1, -1: -1, -2: -1, -3: -1},
    {1: 1, 2: 1, 3: 1, 4: 1, -1: -1, -2: -1, -3: -1},
    {1: 1, 2: 1, 3: 1, 4: 1, -1: -1, -2: -1, -3: -1},
    {1: 1, 2: 1, 3: 1, 4: 1, -1: -1, -2: -1, -3: -1},
    {1: 1, 2: 1, 3: 1, 4: 1, -1: -1, -2: -1, -3: -1},
    {1: 1, 2: 1, 3: 1, 4: 1, -1: -1, -2: -1, -3: -1},
    {1: 1, 2: 1, 3: 1, 4: 1, -1: -1, -2: -1, -3: -1},
)
SUM_SIGN = (1, 1, -1, -1, 1, 1, -1, -1)
SPREAD_TREE = (
    {1: 1, 2: 1, 3: 1, 4: 1, -1: -1, -2: -1, -3: -1},
    {1: 1, 2: 1, 3: 1, 4: 1, -1: -1, -2: -1, -3: -1},
    {1: 1, 2: 1, 3: 1, 4: 1, -1: -1, -2: -1, -3: -1},
    {1: 1, 2: 1, 3: 1, 4: 1, -1: -1, -2: -1, -3: -1},
)
SPREAD_SIGN = (1, -1, 1, -1)
ORDER = (
    ("Y",), ("I",), ("G", 1, 0), ("G", 3, 0), ("G", 2, 0), ("G", 12, 0),
    ("F", 0, 0), ("R", 0, 4), ("R", 0, -3), ("G", 1, 1), ("G", 3, 1), ("G", 12, 1),
    ("G", 2, 1), ("X", 0), ("F", 0, 3), ("R", 1, 4), ("R", 1, -3), ("G", 4, 0),
    ("G", 6, 0), ("G", 7, 0), ("G", 5, 0), ("R", 0, 3), ("R", 0, -2), ("F", 1, 0),
    ("X", 1), ("R", 1, -2), ("G", 5, 1), ("G", 13, 0), ("G", 7, 1), ("R", 1, 3),
    ("R", 2, 4), ("R", 2, -3), ("G", 14, 0), ("R", 0, 2), ("R", 0, -1), ("G", 4, 1),
    ("G", 6, 1), ("G", 11, 0), ("G", 15, 0), ("F", 1, 3), ("R", 1, -1), ("R", 1, 2),
    ("R", 3, 4), ("R", 3, -3), ("F", 3, 0), ("G", 13, 1), ("G", 14, 1), ("R", 6, 4),
    ("R", 2, -2), ("R", 6, -3), ("R", 2, 3), ("R", 0, 1), ("X", 3), ("G", 11, 1),
    ("G", 15, 1), ("G", 10, 0), ("F", 3, 3), ("R", 1, 1), ("R", 7, 4), ("R", 3, 3),
    ("R", 7, -3), ("R", 3, -2), ("G", 8, 0), ("G", 9, 0), ("R", 6, 3), ("R", 2, -1),
    ("G", 10, 1), ("R", 2, 2), ("R", 6, -2), ("F", 2, 0), ("R", 4, -3), ("R", 4, 4),
    ("X", 2), ("G", 8, 1), ("A", 0), ("R", 7, 3), ("G", 9, 1), ("R", 7, -2),
    ("R", 3, 2), ("R", 3, -1), ("R", 6, 2), ("F", 2, 3), ("R", 5, 4), ("R", 5, -3),
    ("R", 2, 1), ("R", 6, -1), ("R", 4, -2), ("R", 4, 3), ("Z", 0, 1), ("Z", 0, -1),
    ("R", 7, 2), ("R", 7, -1), ("R", 3, 1), ("R", 5, 3), ("R", 6, 1), ("R", 5, -2),
    ("R", 4, 2), ("R", 4, -1), ("Z", 0, -2), ("Z", 0, 2), ("R", 5, 2), ("R", 7, 1),
    ("A", 1), ("R", 4, 1), ("R", 5, -1), ("Z", 0, -3), ("R", 5, 1), ("Z", 0, 3),
    ("A", 3), ("Z", 1, 1), ("Z", 1, -1), ("A", 2), ("Z", 0, 4), ("C", 0),
    ("S", 0), ("Z", 3, 1), ("Z", 3, -1), ("Z", 1, 2), ("O", 0), ("Z", 1, -2),
    ("T", 2), ("Z", 2, -1), ("Z", 2, 1), ("Z", 3, 2), ("Z", 3, -2), ("Z", 1, 3),
    ("Z", 1, -3), ("Z", 2, -2), ("Z", 2, 2), ("Z", 3, 3), ("Z", 3, -3), ("Z", 1, 4),
    ("C", 1), ("S", 1), ("W", 1, 4), ("W", 1, 3), ("W", 1, 5), ("W", 0, 5),
    ("Z", 2, 3), ("Z", 2, -3), ("O", 1), ("T", 6), ("T", 4), ("Z", 3, 4),
    ("C", 3), ("S", 3), ("W", 0, 4), ("W", 1, 0), ("W", 0, 0), ("W", 1, 1),
    ("O", 3), ("T", 12), ("T", 15), ("T", 13), ("Z", 2, 4), ("C", 2),
    ("S", 2), ("W", 2, 4), ("W", 3, 4), ("W", 2, 0), ("W", 3, 0), ("O", 2),
    ("T", 10), ("T", 3), ("T", 9), ("T", 8), ("T", 11), ("W", 2, 5),
    ("W", 3, 5), ("T", 1), ("W", 0, 3), ("W", 2, 3), ("W", 3, 3), ("W", 1, 2),
    ("W", 0, 2), ("W", 2, 2), ("W", 3, 2), ("W", 0, 1), ("W", 2, 1), ("W", 3, 1),
    ("T", 7), ("T", 14), ("T", 5), ("E",),
)
SLOT = {p: i for i, p in enumerate(p for chunk in CHUNK_PIECES for p in chunk)}
OWN = SLOT[0, 0]


def less(p, d):
    return tuple((a - b + 1) % 4 - 1 for a, b in zip(p, d))


SOURCE = {p: less(p, d) for p, d in GATHER}
COMES = dict(GATHER)
PARENT = {p: less(p, d) for p, d in REDUCE.items()}
CHILDREN = {p: [q for q in REDUCE if PARENT[q] == p] for p in SLOT}
PIECES = {s: p for p, s in SLOT.items()}
OFFSETS = (1, 2, 3, 4, -1, -2, -3)
NT = (((1,), (1,)), ((), ()))
W_ORDER = [step[1] for step in ORDER if step[0] == "W" and step[2] == 0]


def dot(a, b, dims=(((1,), (0,)), ((), ()))):
    return lax.dot_general(a, b, dims, preferred_element_type=F32)


def kernel(
    x_hbm, wg_hbm, wu_hbm, wd_hbm, c_hbm,
    gi_out, gg_out, gu_out, gd_out,
    own, stage, xc, xt, wcat, wt, wd, part, gu_s, gu_r, dh_s, dh_r, agb, act, ht,
    gi_own, gi_s, gi_r, tr_s, tr_r, fin, acc_gu, acc_d,
    load_sem, stage_sem, ag_ss, ag_rs, sib_ss, sib_rs, rs_ss, rs_rs, za_ss, za_rs,
    gx_ss, gx_rs, tr_ss, tr_rs, fin_sem,
):
    z = lax.axis_index("mp")
    h = lax.axis_index("hidden")
    c = lax.rem(h, 2)
    chip = h // 2
    x, y = lax.rem(chip, NX), chip // NX

    def at(d):
        nx, ny = lax.rem(x + d[0] + NX, NX), lax.rem(y + d[1] + NY, NY)
        return {"hidden": (ny * NX + nx) * 2 + c}

    sibling = {"hidden": h + 1 - 2 * c}

    def zat(o):
        return lax.rem(z + o + NZ, NZ)

    def send(src, dst, ss, rs, dev):
        return pltpu.make_async_remote_copy(
            src_ref=src, dst_ref=dst, send_sem=ss, recv_sem=rs, device_id=dev, device_id_type=MESH
        )

    sent = []

    def start(copy):
        copy.start()
        sent.append(copy)

    loads = [
        pltpu.make_async_copy(x_hbm, own.at[0], load_sem.at[0]),
        pltpu.make_async_copy(c_hbm, own.at[1], load_sem.at[1]),
        pltpu.make_async_copy(wg_hbm, wcat.at[:, pl.ds(0, FD)], load_sem.at[2]),
        pltpu.make_async_copy(wu_hbm, wcat.at[:, pl.ds(FD, FD)], load_sem.at[3]),
        pltpu.make_async_copy(wd_hbm, wd, load_sem.at[4]),
    ]
    for copy in loads:
        copy.start()

    reach = sorted({d for d in COMES.values()} | {(-a, -b) for a, b in COMES.values()}
                   | set(REDUCE.values()) | {(-a, -b) for a, b in REDUCE.values()})
    reach = sorted({((a + 1) % 4 - 1, (b + 1) % 4 - 1) for a, b in reach})
    along = sorted({s * d for tree in SUM_TREE + SPREAD_TREE for d in tree.values() for s in (1, -1)})
    greet = [at(d) for d in reach] + [{"mp": zat(d)} for d in along] + [sibling]
    barrier = pltpu.get_barrier_semaphore()
    for dev in greet:
        pl.semaphore_signal(barrier, inc=1, device_id=dev, device_id_type=MESH)
    pl.semaphore_wait(barrier, len(greet))

    ours = pl.ds(pl.multiple_of(c * HALF, 128), HALF)
    theirs = pl.ds(pl.multiple_of((1 - c) * HALF, 128), HALF)

    def swap(a):
        return send(own.at[a, :, theirs], stage.at[a], stage_sem.at[0, a], stage_sem.at[1, a], sibling)

    for a in (0, 1):
        loads[a].wait()
        start(swap(a))

    def share(a, s, cols):
        block = xc.at[a, s, :, cols]
        return send(block, block, sib_ss.at[s, a], sib_rs.at[s, a], sibling)

    def hop(p, a):
        s, d = SLOT[p], COMES[p]
        return send(
            xc.at[a, SLOT[SOURCE[p]], :, ours], xc.at[a, s, :, ours],
            ag_ss.at[s, a], ag_rs.at[s, a], at((-d[0], -d[1])),
        )

    def forward(q, a):
        for p, _ in GATHER:
            if SOURCE[p] == q:
                start(hop(p, a))

    def gather(s, a):
        hop(PIECES[s], a).wait_recv()
        forward(PIECES[s], a)
        start(share(a, s, ours))

    def begin(a):
        swap(a).wait_recv()
        mine, other = own[a, :, ours].astype(F32), stage[a].astype(F32)
        first = c == 0
        xc[a, OWN, :, ours] = jnp.concatenate(
            [jnp.where(first, mine, other), jnp.where(first, other, mine)], axis=0
        ).astype(BF16)
        forward((0, 0), a)
        start(share(a, OWN, ours))

    begin(0)

    def flip_weights():
        for copy in loads[2:]:
            copy.wait()

        def tile(n, _):
            cols = pl.ds(pl.multiple_of(n * 256, 256), 256)
            wt[:, cols] = wcat[cols, :].T
            return 0

        lax.fori_loop(0, DM // 256, tile, 0)

    def flip_inputs(k):
        def tile(n, _):
            cols = pl.ds(pl.multiple_of(n * 256, 256), 256)
            xt[k, cols, pl.ds(0, ROWS)] = xc[0, pl.ds(PER * k, PER), :, cols].reshape(ROWS, 256).T
            return 0

        lax.fori_loop(0, DM // 256, tile, 0)

    def rows_of(a, k):
        return xc[a, pl.ds(PER * k, PER)].reshape(ROWS, DM)

    def product(k, n):
        a = 0 if n == 0 else 1
        for i in range(PER * k, PER * k + PER):
            share(a, i, theirs).wait_recv()
        if n == 0:
            part[k, :, :, pl.ds(0, 2 * FD)] = dot(rows_of(0, k), wcat[...]).reshape(NZ, BLK, 2 * FD)
        else:
            part[k, :, :, pl.ds(2 * FD, FD)] = dot(rows_of(1, k), wd[...], NT).reshape(NZ, BLK, FD)

    def sum_copy(u, o):
        k, j, m = u // 2, u % 2, OFFSETS.index(o)
        src, dst = (dh_s, dh_r) if j else (gu_s, gu_r)
        dev = {"mp": zat(SUM_SIGN[u] * SUM_TREE[u][o])}
        return send(src.at[k, m], dst.at[k, m], rs_ss.at[u, m], rs_rs.at[u, m], dev)

    def sum_at(u, o):
        k, j = u // 2, u % 2
        cols, landed = (pl.ds(2 * FD, FD), dh_r) if j else (pl.ds(0, 2 * FD), gu_r)
        value = part[k, zat(SUM_SIGN[u] * o), :, cols]
        for q, d in SUM_TREE[u].items():
            if q - d == o:
                sum_copy(u, q).wait_recv()
                value = value + landed[k, OFFSETS.index(q)].astype(F32)
        return value

    def reduce(u, o):
        (dh_s if u % 2 else gu_s)[u // 2, OFFSETS.index(o)] = sum_at(u, o).astype(BF16)
        start(sum_copy(u, o))

    def spread_copy(k, o):
        m, d = OFFSETS.index(o), SPREAD_TREE[k][o]
        block = agb.at[k, zat(SPREAD_SIGN[k] * (o - d))]
        return send(block, block, za_ss.at[k, m], za_rs.at[k, m], {"mp": zat(-SPREAD_SIGN[k] * d)})

    def spread_wait(k, o):
        m, d = OFFSETS.index(o), SPREAD_TREE[k][o]
        block = agb.at[k, zat(SPREAD_SIGN[k] * o)]
        send(block, block, za_ss.at[k, m], za_rs.at[k, m], {"mp": zat(-SPREAD_SIGN[k] * d)}).wait_recv()

    def spread_on(k, q):
        for o, d in SPREAD_TREE[k].items():
            if o - d == q:
                start(spread_copy(k, o))

    def spread(k, o):
        spread_wait(k, o)
        spread_on(k, o)

    def activate(k):
        both, dhid = sum_at(2 * k, 0), sum_at(2 * k + 1, 0)
        gate, up = both[:, :FD], both[:, FD:]
        sig = jax.nn.sigmoid(gate)
        agb[k, z] = jnp.concatenate(
            [
                gate * sig * up,
                dhid * up * sig * (1.0 + gate * (1.0 - sig)),
                dhid * gate * sig,
            ],
            axis=1,
        ).astype(BF16)
        spread_on(k, 0)

    def collect(k):
        act[k] = jnp.concatenate([agb[k, j].astype(F32) for j in range(NZ)], axis=0).astype(BF16)
        ht[k, :, pl.ds(0, ROWS)] = act[k, :, pl.ds(0, FD)].T

    def gi_swap(k):
        s = pl.ds(PER * k, PER)
        return send(gi_s.at[s], gi_r.at[s], gx_ss.at[k], gx_rs.at[k], sibling)

    def input_grad(k, half, dst):
        cols = pl.ds(pl.multiple_of(half * HALF, 128), HALF)
        value = dot(act[k, :, pl.ds(FD, 2 * FD)], wt[:, cols])
        dst[pl.ds(PER * k, PER)] = value.reshape(PER, PIECE, HALF).astype(dst.dtype)

    def their_half(k):
        input_grad(k, 1 - c, gi_s)
        start(gi_swap(k))

    def our_half(k):
        input_grad(k, c, gi_own)
        gi_swap(k).wait_recv()

    def tr_copy(p):
        s = SLOT[p]
        return send(tr_s.at[s], tr_r.at[s], tr_ss.at[s], tr_rs.at[s], at(REDUCE[p]))

    def tree_sum(p):
        s = SLOT[p]
        value = gi_own[s] + gi_r[s].astype(F32)
        for q in CHILDREN[p]:
            tr_copy(q).wait_recv()
            value = value + tr_r[SLOT[q]].astype(F32)
        return value

    def tree(s):
        tr_s[s] = tree_sum(PIECES[s]).astype(BF16)
        start(tr_copy(PIECES[s]))

    def weight_grads(k, i):
        last = k == W_ORDER[-1]
        slots = pl.ds(PER * k, PER)

        cols = pl.ds(DM // 3 * (i % 3), DM // 3)
        if i < 3:
            value = dot(xt[k, cols, pl.ds(0, ROWS)], act[k, :, pl.ds(FD, 2 * FD)])
            if k != W_ORDER[0]:
                value = value + acc_gu[cols, :]
            if last:
                gg_out[cols, :] = value[:, :FD].astype(BF16)
                gu_out[cols, :] = value[:, FD:].astype(BF16)
            else:
                acc_gu[cols, :] = value
        else:
            value = dot(ht[k, :, pl.ds(0, ROWS)], xc[1, slots, :, cols].reshape(ROWS, DM // 3))
            if k != W_ORDER[0]:
                value = value + acc_d[:, cols]
            if last:
                gd_out[:, cols] = value.astype(BF16)
            else:
                acc_d[:, cols] = value

    def finish():
        for copy in sent:
            copy.wait_send()
        sent.clear()
        gi_own[OWN] = tree_sum((0, 0))
        sent_rows = pl.ds(pl.multiple_of((1 - c) * SHARD, 8), SHARD)
        kept_rows = pl.ds(pl.multiple_of(c * SHARD, 8), SHARD)
        fin[1] = gi_own[OWN, sent_rows, :].astype(BF16)
        copy = send(fin.at[1], fin.at[0], fin_sem.at[0], fin_sem.at[1], sibling)
        start(copy)
        gi_out[:, ours] = gi_own[OWN, kept_rows, :].astype(BF16)
        copy.wait_recv()
        gi_out[:, theirs] = fin[0]

    steps = {
        "G": gather, "F": product, "R": reduce, "A": activate, "Z": spread, "C": collect,
        "S": their_half, "O": our_half, "T": tree, "W": weight_grads, "E": finish, "X": flip_inputs, "Y": flip_weights,
        "I": lambda: begin(1),
    }
    for step, *numbers in ORDER:
        steps[step](*numbers)
    for copy in sent:
        copy.wait_send()


def store(*refs):
    n = len(refs) // 2
    copies = [pltpu.make_async_copy(refs[i], refs[n + i], refs[-1].at[i]) for i in range(n)]
    for copy in copies:
        copy.start()
    for copy in copies:
        copy.wait()


def shards(inputs, gate_weight, up_weight, down_weight, cotangent):
    dma = pltpu.SemaphoreType.DMA
    any_spec = pl.BlockSpec(memory_space=pl.ANY)
    slots, offsets = CHUNKS * PER, len(OFFSETS)
    shapes = ((SHARD, DM), (DM, FD), (DM, FD), (FD, DM))
    results = pl.pallas_call(
        kernel,
        out_shape=tuple(pltpu.VMEM(shape, BF16) for shape in shapes),
        in_specs=[any_spec] * 5,
        out_specs=(pl.BlockSpec(memory_space=pltpu.VMEM),) * 4,
        scratch_shapes=[
            pltpu.VMEM((2, SHARD, DM), BF16),
            pltpu.VMEM((2, SHARD, HALF), BF16),
            pltpu.VMEM((2, slots, PIECE, DM), BF16),
            pltpu.VMEM((CHUNKS, DM, 256), BF16),
            pltpu.VMEM((DM, 2 * FD), BF16),
            pltpu.VMEM((2 * FD, DM), BF16),
            pltpu.VMEM((FD, DM), BF16),
            pltpu.VMEM((CHUNKS, NZ, BLK, 3 * FD), F32),
            pltpu.VMEM((CHUNKS, offsets, BLK, 2 * FD), BF16),
            pltpu.VMEM((CHUNKS, offsets, BLK, 2 * FD), BF16),
            pltpu.VMEM((CHUNKS, offsets, BLK, FD), BF16),
            pltpu.VMEM((CHUNKS, offsets, BLK, FD), BF16),
            pltpu.VMEM((CHUNKS, NZ, BLK, 3 * FD), BF16),
            pltpu.VMEM((CHUNKS, ROWS, 3 * FD), BF16),
            pltpu.VMEM((CHUNKS, FD, 256), BF16),
            pltpu.VMEM((slots, PIECE, HALF), F32),
            pltpu.VMEM((slots, PIECE, HALF), BF16),
            pltpu.VMEM((slots, PIECE, HALF), BF16),
            pltpu.VMEM((slots, PIECE, HALF), BF16),
            pltpu.VMEM((slots, PIECE, HALF), BF16),
            pltpu.VMEM((2, SHARD, HALF), BF16),
            pltpu.VMEM((DM, 2 * FD), F32),
            pltpu.VMEM((FD, DM), F32),
            dma((5,)),
            dma((2, 2)),
            dma((slots, 2)), dma((slots, 2)),
            dma((slots, 2)), dma((slots, 2)),
            dma((2 * CHUNKS, offsets)), dma((2 * CHUNKS, offsets)),
            dma((CHUNKS, offsets)), dma((CHUNKS, offsets)),
            dma((CHUNKS,)), dma((CHUNKS,)),
            dma((slots,)), dma((slots,)),
            dma((2,)),
        ],
        compiler_params=pltpu.CompilerParams(
            collective_id=0, has_side_effects=True, vmem_limit_bytes=57 * 1024 * 1024
        ),
    )(inputs, gate_weight, up_weight, down_weight, cotangent)
    return pl.pallas_call(
        store,
        out_shape=tuple(jax.ShapeDtypeStruct(shape, BF16) for shape in shapes),
        in_specs=[pl.BlockSpec(memory_space=pltpu.VMEM)] * 4,
        out_specs=(any_spec,) * 4,
        scratch_shapes=[dma((4,))],
        compiler_params=pltpu.CompilerParams(vmem_limit_bytes=1024 * 1024),
    )(*(pltpu.with_memory_space_constraint(a, pltpu.VMEM) for a in results))


def solution(mesh):
    placed = (
        P("hidden", "mp"),
        P("mp", "hidden"),
        P("mp", "hidden"),
        P("hidden", "mp"),
        P("hidden", "mp"),
    )
    return jax.shard_map(
        shards,
        mesh=mesh,
        in_specs=placed,
        out_specs=(P("hidden", "mp"), P("mp", "hidden"), P("mp", "hidden"), P("hidden", "mp")),
        check_vma=False,
    )
```
